512 devices in a mesh: dp: 128 (over y, z, core), proto: 4 (over x).
Axes of the slice: x: 4, y: 8, z: 8, core: 2. Of those that a mesh axis runs over, the one named last changes fastest.
Arguments:
- embeddings: bfloat16 [2, 16384, 256], P(None, 'dp'), may hold values from -8 to 8
- prototypes: bfloat16 [256, 16384], P(None, 'proto'), may hold values from -0.375 to 0.375
Outputs:
- grad_embeddings: float32 [2, 16384, 256], P(None, 'dp')
- grad_prototypes: float32 [256, 16384], P('dp', 'proto')
The draws below stay inside these ranges and needn't reach their ends.
All inputs are finite; a program needn't handle non-finite values.
Results may differ from the reference program's by a relative error of at most 0.0041.
The reference program's roundings to bfloat16 on the way count: a program that leaves them out, or rounds other values in their place, can miss the bound.
Values sent between devices are 32-bit elements; how exact they have to be, the bound alone decides.
A program may use at most 64 MiB of HBM per device.

```python
import math
import jax
import jax.numpy as jnp
from jax import lax

D = 256
K = 16384
TOK_DEV = 128
ITERS = 2
TOKENS = 16384
N_DP = 128


def draw_embeddings(key, part):
    key = jax.random.fold_in(key, 7)
    subkeys = jax.random.split(key, 5)
    direction = jax.random.normal(subkeys[0], (D,), jnp.float32)
    user_part = jax.random.normal(subkeys[1], (TOKENS, D), jnp.float32)
    jitter = jax.random.normal(subkeys[2], (2, TOKENS, D), jnp.float32)
    lowest = 0.3
    highest = 3.0
    strength = jnp.exp(jax.random.uniform(subkeys[3], (TOKENS, 1), jnp.float32, math.log(lowest), math.log(highest)))
    position = jnp.arange(TOKENS, dtype=jnp.float32)[:, None]
    ramp_scale = 0.5 + 1.5 * position / TOKENS
    pairing = jax.random.permutation(subkeys[4], N_DP)
    row_owner = jnp.arange(TOKENS) // TOK_DEV
    feature_block = jnp.arange(D) // (D // N_DP)
    booster = jnp.where(pairing[row_owner][:, None] == feature_block[None, :], 4.0, 1.0)
    values = (strength * ramp_scale * direction + user_part + 0.7 * jitter) * booster / 32.0
    return jnp.clip(values, -8.0, 8.0).astype(jnp.bfloat16)


def shard_levels(own_key, extent, cuts, smallest, top_value):
    def one(dim, blocks):
        heights = jax.random.uniform(jax.random.fold_in(jax.random.fold_in(own_key, 6), dim), (blocks,), jnp.float32, smallest / len(cuts), top_value / len(cuts))
        return jnp.repeat(jnp.exp(heights), extent[dim] // blocks).reshape((-1,) + (1,) * (len(extent) - dim - 1))

    level = one(*cuts[0])
    for cut in cuts[1:]:
        level = level * one(*cut)
    return level


def noise(rng, shape, scale, limit, pieces=(), kind=jnp.bfloat16):
    gain = shard_levels(rng, shape, pieces, -0.22, 0.18) if pieces else 1.0
    drawn = jax.random.normal(rng, shape, jnp.float32) * scale * gain
    return jnp.minimum(jnp.maximum(drawn, -limit), limit).astype(kind)


def setup_inputs(seed: int = 0) -> dict:
    splits = jax.random.split(jax.random.key(seed), 3)
    return {
        "embeddings": draw_embeddings(jax.random.fold_in(splits[2], 71), 0),
        "prototypes": noise(splits[1], (D, K), D ** -0.5, 0.375, ((1, 4),)),
    }


sharpness_for_codebook = 0.05
guess_heat_inverse = 0.1

def unit_embed(values):
    return values * lax.rsqrt(lax.optimization_barrier(jnp.mean(values * values, axis=-1, keepdims=True)) + 1e-06) * values.shape[-1] ** (-0.5)

def unit_protos(prototypes):
    wide = prototypes.astype(jnp.float32)
    scaled = wide * lax.rsqrt(lax.optimization_barrier(jnp.mean(wide * wide, axis=0, keepdims=True)) + 1e-06) * wide.shape[0] ** (-0.5)
    return scaled.astype(jnp.bfloat16)

def tile_affinities(present_sample_tile, collected_centroids):
    return jnp.einsum('vrd,dk->vrk', present_sample_tile.astype(jnp.float32), collected_centroids)

def reference(embeddings, prototypes):
    embed_wide = embeddings.astype(jnp.float32)
    unit_wide, pull_back = jax.vjp(unit_embed, embed_wide)
    unit_half = unit_wide.astype(jnp.bfloat16)
    proto_unit = unit_protos(prototypes)
    collected_centroids = proto_unit.astype(jnp.float32)
    row_blocks = unit_half.reshape(2, N_DP, TOK_DEV, D).transpose(1, 0, 2, 3)

    def kernel_of(present_sample_tile):
        return jnp.exp(tile_affinities(present_sample_tile, collected_centroids) / sharpness_for_codebook)
    row_scaling = jnp.ones((N_DP, 2, TOK_DEV), jnp.float32)
    column_scaling = jnp.ones((2, K), jnp.float32)
    for sweep in range(ITERS):

        def column_step(running, inputs):
            present_sample_tile, scale_block = inputs
            exponentiated_affinity = kernel_of(present_sample_tile)
            return (running + lax.optimization_barrier(jnp.sum(exponentiated_affinity * scale_block[:, :, None], axis=1)), None)
        column_total, unused = lax.scan(column_step, jnp.zeros((2, K), jnp.float32), (row_blocks, row_scaling))
        column_scaling = 1.0 / column_total

        def row_step(present_sample_tile):
            exponentiated_affinity = kernel_of(present_sample_tile)
            return lax.optimization_barrier(jnp.sum(exponentiated_affinity * column_scaling[:, None, :], axis=-1))
        row_scaling = 1.0 / lax.map(row_step, row_blocks)

    def final_step(running, inputs):
        present_sample_tile, scale_block = inputs
        anchor_resemblances = tile_affinities(present_sample_tile, collected_centroids)
        exponentiated_affinity = jnp.exp(anchor_resemblances / sharpness_for_codebook)
        wanted_group_soft_marks = scale_block[:, :, None] * exponentiated_affinity * column_scaling[:, None, :]
        anchor_vectors = jnp.exp(anchor_resemblances / guess_heat_inverse)
        guessed_chances = anchor_vectors / lax.optimization_barrier(jnp.sum(anchor_vectors, axis=-1, keepdims=True))
        resemblance_sensitivity = ((guessed_chances - wanted_group_soft_marks[::-1]) / guess_heat_inverse).astype(jnp.bfloat16)
        grad_wide = resemblance_sensitivity.astype(jnp.float32)
        grad_block = jnp.einsum('vrk,dk->vrd', grad_wide, collected_centroids)
        running = running + jnp.einsum('vrd,vrk->dk', present_sample_tile.astype(jnp.float32), grad_wide)
        return (running, grad_block)
    grad_prototypes, grad_blocks = lax.scan(final_step, jnp.zeros((D, K), jnp.float32), (row_blocks, row_scaling))
    grad_unit = grad_blocks.transpose(1, 0, 2, 3).reshape(2, TOKENS, D)
    grad_embeddings = pull_back(grad_unit)[0]
    return (grad_embeddings, grad_prototypes)
```

```python
import jax
import jax.numpy as jnp
from jax import lax
from jax.experimental import pallas as pl
from jax.experimental.pallas import tpu as pltpu
from jax.sharding import PartitionSpec as P

MESH = pl.DeviceIdType.MESH
F32 = jnp.float32
BF16 = jnp.bfloat16

RING = 8
XS = 4
D = 256
COLS = 2048
HALF = 1024
CH = 512
ORDER = (4, 3, 5, 2, 6, 1, 7)


def place():
    dp = lax.axis_index("dp")
    x = lax.axis_index("proto")
    return lax.div(dp, 16), lax.rem(lax.div(dp, 2), RING), lax.rem(dp, 2), x


def device(y, z, c, x):
    return (y * 16 + z * 2 + c, x)


def kernel(
    emb_ref,
    proto_ref,
    ge_ref,
    gp_ref,
    praw,
    pn,
    usend,
    urecv,
    uall,
    ut,
    e_ref,
    cpart,
    csend,
    crecv,
    cvec,
    racc,
    rsend,
    rrecv,
    rb,
    zb,
    g_ref,
    gpart,
    rs_recv,
    p2send,
    p2recv,
    fin,
    fin_recv,
    gu_send,
    gu_recv,
    gx,
    gx_recv,
    gef,
    psem,
    ssem,
    rsem,
):
    y, z, c, x = place()
    used = [0]
    ends = []

    def sem():
        used[0] += 1
        return used[0] - 1

    def along(axis, s):
        if axis == "y":
            return device(lax.rem(y + s, RING), z, c, x)
        return device(y, lax.rem(z + s, RING), c, x)

    sibling = device(y, z, 1 - c, x)

    def remote(src, dst, k, target):
        return pltpu.make_async_remote_copy(
            src_ref=src,
            dst_ref=dst,
            send_sem=ssem.at[k],
            recv_sem=rsem.at[k],
            device_id=target,
            device_id_type=MESH,
        )

    def send(src, dst, target):
        k = sem()
        copy = remote(src, dst, k, target)
        copy.start()
        ends.append(copy.wait_send)
        return copy.wait_recv

    def fan(parts, whole):
        k = sem()
        for src, dst, target in parts:
            remote(src, dst, k, target).start()
        ends.append(lambda: pltpu.make_async_copy(whole, whole, ssem.at[k]).wait())
        return lambda: pltpu.make_async_copy(whole, whole, rsem.at[k]).wait()

    load = pltpu.make_async_copy(
        proto_ref.at[:, pl.ds(pl.multiple_of(c * COLS, COLS), COLS)], praw, psem
    )
    load.start()

    row_peers = [(s // 2, s % 2) for s in range(1, 2 * XS)]

    def row_peer(dx, dc):
        return device(y, z, lax.rem(c + dc, 2), lax.rem(x + dx, XS))

    barrier = pltpu.get_barrier_semaphore()
    peers = [along("y", s) for s in ORDER] + [along("z", s) for s in ORDER]
    peers += [row_peer(*p) for p in row_peers]
    for target in peers:
        pl.semaphore_signal(barrier, inc=1, device_id=target, device_id_type=MESH)

    def unit_rows(i, carry):
        wide = emb_ref[i].astype(F32)
        inv = lax.rsqrt(jnp.mean(wide * wide, axis=-1, keepdims=True) + 1e-06)
        half = (wide * inv * 0.0625).astype(BF16)
        rows = pl.ds(pl.multiple_of(i * 64, 64), 64)
        usend[rows, :] = half.astype(F32)
        uall[c, rows, :] = half
        return carry

    lax.fori_loop(0, 4, unit_rows, 0)
    load.wait()

    def unit_protos(i, carry):
        cols = pl.ds(pl.multiple_of(i * 256, 256), 256)
        wide = praw[:, cols].astype(F32)
        inv = lax.rsqrt(jnp.mean(wide * wide, axis=0, keepdims=True) + 1e-06)
        pn[:, cols] = (wide * inv * 0.0625).astype(BF16)
        return carry

    lax.fori_loop(0, COLS // 256, unit_protos, 0)

    def scores(slot, first):
        for v in range(2):
            def step(i, carry):
                cols = pl.ds(pl.multiple_of(i * 256, 256), 256)
                s = jnp.dot(
                    uall[slot, v * 128 : (v + 1) * 128, :], pn[:, cols], preferred_element_type=F32
                )
                e = jnp.exp(s * 10.0)
                e_ref[slot, v * 128 : (v + 1) * 128, cols] = e
                k = jnp.sum((e * e).reshape(16, 8, 256), axis=0)
                if first:
                    cpart[v, :, cols] = k
                else:
                    cpart[v, :, cols] += k
                return carry

            lax.fori_loop(0, COLS // 256, step, 0)

    scores(c, True)
    pl.semaphore_wait(barrier, len(peers))
    got_u = send(usend, urecv, sibling)
    got_u()
    uall[1 - c] = urecv[...].astype(BF16)
    scores(1 - c, False)

    def put_columns(it):
        for h in range(2):
            for v in range(2):
                csend[it, 0, h, v : v + 1, :] = jnp.sum(
                    cpart[v, :, h * HALF : (h + 1) * HALF], axis=0, keepdims=True
                )

    def columns(it):
        waits = []

        def go(ph, h):
            axis = "y" if (ph + h) % 2 == 0 else "z"
            return fan(
                [
                    (csend.at[it, ph, h], crecv.at[it, ph, h, s - 1], along(axis, s))
                    for s in ORDER
                ],
                crecv.at[it, ph, h],
            )

        for h in range(2):
            waits.append(go(0, h))
        again = []
        for h in range(2):
            waits[h]()
            total = csend[it, 0, h]
            for s in range(RING - 1):
                total = total + crecv[it, 0, h, s]
            csend[it, 1, h] = total
            again.append(go(1, h))
        for h in range(2):
            again[h]()
            total = csend[it, 1, h]
            for s in range(RING - 1):
                total = total + crecv[it, 1, h, s]
            cvec[:, h * HALF : (h + 1) * HALF] = 1.0 / total

    def row_pass(it):
        for slot in range(2):
            for v in range(2):
                def step(i, carry):
                    rows = pl.ds(pl.multiple_of(v * 128 + i * 32, 32), 32)
                    acc = jnp.zeros((32, 128), F32)
                    tot = jnp.zeros((32, 128), F32)
                    for t in range(COLS // 128):
                        e = e_ref[slot, rows, t * 128 : (t + 1) * 128]
                        acc = acc + e * e * cvec[v : v + 1, t * 128 : (t + 1) * 128]
                        if it == 0:
                            tot = tot + e
                    racc[0, slot * 2 + v, pl.ds(pl.multiple_of(i * 32, 32), 32), :] = acc
                    if it == 0:
                        racc[1, slot * 2 + v, pl.ds(pl.multiple_of(i * 32, 32), 32), :] = tot
                    return carry

                lax.fori_loop(0, 4, step, 0)
        for w in range(2):
            for q in range(4):
                if it == 0 or w == 0:
                    row = jnp.sum(racc[w, q].T, axis=0, keepdims=True)
                else:
                    row = jnp.zeros((1, 128), F32)
                rsend[it, w * 4 + q : w * 4 + q + 1, :] = row

    def row_exchange(it):
        got = fan(
            [(rsend.at[it], rrecv.at[it, i], row_peer(*p)) for i, p in enumerate(row_peers)],
            rrecv.at[it],
        )
        got()
        total = rsend[it]
        for i in range(len(row_peers)):
            total = total + rrecv[it, i]
        scale = 1.0 / total
        for q in range(4):
            rb[q] = jnp.broadcast_to(scale[q : q + 1, :], (128, 128)).T
            if it == 0:
                zb[q] = jnp.broadcast_to(scale[4 + q : 5 + q, :], (128, 128)).T

    def column_pass():
        def step(i, carry):
            base = i * 512
            for v in range(2):
                acc = [jnp.zeros((8, 128), F32) for _ in range(4)]

                def rows8(j, acc):
                    acc = list(acc)
                    for slot in range(2):
                        for w in range(2):
                            r0 = pl.multiple_of(j * 16 + w * 8, 8)
                            r = rb[slot * 2 + v, pl.ds(r0, 8), :]
                            for t in range(4):
                                cols = pl.ds(pl.multiple_of(base + t * 128, 128), 128)
                                e = e_ref[slot, pl.ds(pl.multiple_of(v * 128 + r0, 8), 8), cols]
                                acc[t] = acc[t] + e * e * r
                    return tuple(acc)

                acc = lax.fori_loop(0, 8, rows8, tuple(acc))
                for t in range(4):
                    cols = pl.ds(pl.multiple_of(base + t * 128, 128), 128)
                    cpart[v, :, cols] = acc[t]
            return carry

        lax.fori_loop(0, COLS // 512, step, 0)

    put_columns(0)
    columns(0)
    row_pass(0)
    row_exchange(0)
    column_pass()
    put_columns(1)
    columns(1)
    row_pass(1)

    to = lax.broadcasted_iota(jnp.int32, (D, D), 0)
    at = lax.broadcasted_iota(jnp.int32, (D, D), 1)
    natural = (to == at).astype(BF16)
    swapped = ((to // 32) * 4 + ((to // 4) % 8) * 32 + to % 4 == at).astype(BF16)
    for h, order in ((0, natural), (1, swapped)):
        for slot in range(2):
            ut[h, :, slot * 256 : (slot + 1) * 256] = lax.dot_general(
                order, uall[slot], (((1,), (1,)), ((), ())), preferred_element_type=F32
            ).astype(BF16)

    row_exchange(1)

    chunks = [
        ("y", "z", 0, 0, 4, 3),
        ("z", "y", 1, HALF, 4, 3),
        ("y", "z", 0, CH, 3, 4),
        ("z", "y", 1, HALF + CH, 3, 4),
    ]
    own = {"y": y, "z": z}

    def slab(ch, axis, s):
        which = lax.rem(own[axis] + (s + RING), RING)
        return gpart.at[ch, pl.ds(pl.multiple_of(which * 32, 32), 32), :]

    def slot_of(ch, sign, i):
        return i if sign > 0 else chunks[ch][4] + i

    flight = {}

    def hop(ch, sign, i, src):
        axis = chunks[ch][0]
        flight[ch, sign, i] = send(
            src, rs_recv.at[ch, slot_of(ch, sign, i)], along(axis, sign % RING)
        )

    for ch, (axis, _, h, col0, plus, minus) in enumerate(chunks):
        for slot in range(2):
            def step(i, carry):
                r0 = pl.multiple_of(i * 16, 16)
                rows0 = pl.ds(r0, 16)
                rows1 = pl.ds(pl.multiple_of(128 + r0, 16), 16)
                ra = rb[slot * 2, rows0, :] * 10.0
                rc = rb[slot * 2 + 1, rows0, :] * 10.0
                za = zb[slot * 2, rows0, :] * 10.0
                zc = zb[slot * 2 + 1, rows0, :] * 10.0
                for t in range(CH // 128):
                    cols = slice(col0 + t * 128, col0 + (t + 1) * 128)
                    e0 = e_ref[slot, rows0, cols]
                    e1 = e_ref[slot, rows1, cols]
                    k0 = e0 * e0 * cvec[0:1, cols]
                    k1 = e1 * e1 * cvec[1:2, cols]
                    g_ref[slot, rows0, cols] = (e0 * za - k1 * rc).astype(BF16)
                    g_ref[slot, rows1, cols] = (e1 * zc - k0 * ra).astype(BF16)
                return carry

            lax.fori_loop(0, 8, step, 0)
        gpart[ch] = jnp.dot(
            ut[h, :, 0:256], g_ref[0, :, col0 : col0 + CH], preferred_element_type=F32
        ) + jnp.dot(
            ut[h, :, 256:512], g_ref[1, :, col0 : col0 + CH], preferred_element_type=F32
        )
        hop(ch, 1, 0, slab(ch, axis, plus))
        hop(ch, -1, 0, slab(ch, axis, -minus))

    def back(slot):
        return lax.dot_general(
            g_ref[slot], pn[...], (((1,), (1,)), ((), ())), preferred_element_type=F32
        )

    def advance(i):
        for ch, (axis, _, _, _, plus, minus) in enumerate(chunks):
            for sign, length in ((1, plus), (-1, minus)):
                if i >= length:
                    continue
                flight[ch, sign, i]()
                left = length - 1 - i
                if left:
                    here = rs_recv.at[ch, slot_of(ch, sign, i)]
                    here[...] = here[...] + slab(ch, axis, sign * left)[...]
                    hop(ch, sign, i + 1, here)

    gu_send[...] = back(1 - c)
    got_gu = send(gu_send, gu_recv, sibling)
    gx[...] = back(c).reshape(4, 64, 256)

    advance(0)

    got_gu()
    gx[...] = gx[...] + gu_recv[...].reshape(4, 64, 256)

    def along_x(s):
        return device(y, z, c, lax.rem(x + s, XS))

    got_gx = fan(
        [(gx.at[lax.rem(x + s, XS)], gx_recv.at[s - 1], along_x(s)) for s in (2, 1, 3)], gx_recv
    )

    advance(1)
    advance(2)

    got_gx()
    g = gx[x] + gx_recv[0] + gx_recv[1] + gx_recv[2]
    wide = emb_ref[x].astype(F32)
    inv = lax.rsqrt(jnp.mean(wide * wide, axis=-1, keepdims=True) + 1e-06)
    mean = jnp.mean(wide * g, axis=-1, keepdims=True)
    gef[x] = (g * inv - wide * (inv * inv * inv * mean)) * 0.0625
    got_ge = [send(gef.at[x], gef.at[x], along_x(s)) for s in (2, 1, 3)]

    got_p2 = {}
    for ch, (axis, axis2, _, _, plus, minus) in enumerate(chunks):
        for sign, length in ((1, plus), (-1, minus)):
            if length == 4:
                flight[ch, sign, 3]()
        total = (
            slab(ch, axis, 0)[...]
            + rs_recv[ch, slot_of(ch, 1, plus - 1)]
            + rs_recv[ch, slot_of(ch, -1, minus - 1)]
        )
        for q in range(RING):
            p2send[ch, q] = total[q * 4 : q * 4 + 4, :]
        got_p2[ch] = fan(
            [
                (p2send.at[ch, lax.rem(own[axis2] + s, RING)], p2recv.at[ch, s - 1], along(axis2, s))
                for s in ORDER
            ],
            p2recv.at[ch],
        )

    for wait in got_ge:
        wait()
    ge_ref[...] = gef[...]

    for ch, (_, axis2, _, col0, _, _) in enumerate(chunks):
        got_p2[ch]()
        total = p2send[ch, own[axis2]]
        for s in range(RING - 1):
            total = total + p2recv[ch, s]
        for q in range(2):
            fin[q, :, col0 : col0 + CH] = total[q * 2 : q * 2 + 2, :]
    got_fin = send(fin.at[1 - c], fin_recv, sibling)
    gp_ref[:, pl.ds(pl.multiple_of(c * COLS, COLS), COLS)] = fin[c]
    got_fin()
    gp_ref[:, pl.ds(pl.multiple_of((1 - c) * COLS, COLS), COLS)] = fin_recv[...]

    for wait in ends:
        wait()
    assert used[0] <= SEMS


SEMS = 64


def shards(embeddings, prototypes):
    vmem = pl.BlockSpec(memory_space=pltpu.VMEM)
    ge, gp = pl.pallas_call(
        kernel,
        name="swap_step",
        out_shape=(
            jax.ShapeDtypeStruct((4, 64, D), F32),
            jax.ShapeDtypeStruct((2, 2 * COLS), F32),
        ),
        in_specs=[vmem, pl.BlockSpec(memory_space=pl.ANY)],
        out_specs=(vmem, vmem),
        scratch_shapes=[
            pltpu.VMEM((D, COLS), BF16),
            pltpu.VMEM((D, COLS), BF16),
            pltpu.VMEM((256, D), F32),
            pltpu.VMEM((256, D), F32),
            pltpu.VMEM((2, 256, D), BF16),
            pltpu.VMEM((2, D, 512), BF16),
            pltpu.VMEM((2, 256, COLS), F32),
            pltpu.VMEM((2, 8, COLS), F32),
            pltpu.VMEM((2, 2, 2, 2, HALF), F32),
            pltpu.VMEM((2, 2, 2, RING - 1, 2, HALF), F32),
            pltpu.VMEM((2, COLS), F32),
            pltpu.VMEM((2, 4, 128, 128), F32),
            pltpu.VMEM((2, 8, 128), F32),
            pltpu.VMEM((2, 2 * XS - 1, 8, 128), F32),
            pltpu.VMEM((4, 128, 128), F32),
            pltpu.VMEM((4, 128, 128), F32),
            pltpu.VMEM((2, 256, COLS), BF16),
            pltpu.VMEM((4, D, CH), F32),
            pltpu.VMEM((4, 7, 32, CH), F32),
            pltpu.VMEM((4, RING, 4, CH), F32),
            pltpu.VMEM((4, RING - 1, 4, CH), F32),
            pltpu.VMEM((2, 2, COLS), F32),
            pltpu.VMEM((2, COLS), F32),
            pltpu.VMEM((256, D), F32),
            pltpu.VMEM((256, D), F32),
            pltpu.VMEM((4, 64, D), F32),
            pltpu.VMEM((3, 64, D), F32),
            pltpu.VMEM((4, 64, D), F32),
            pltpu.SemaphoreType.DMA,
            pltpu.SemaphoreType.DMA((SEMS,)),
            pltpu.SemaphoreType.DMA((SEMS,)),
        ],
        compiler_params=pltpu.CompilerParams(
            collective_id=0, has_side_effects=True, vmem_limit_bytes=40 << 20
        ),
        cost_estimate=pl.CostEstimate(
            flops=2_000_000_000, bytes_accessed=4_000_000, transcendentals=1_100_000
        ),
    )(embeddings.reshape(4, 64, D), prototypes)
    return ge.reshape(2, 128, D), gp


def solution(mesh):
    return jax.shard_map(
        shards,
        mesh=mesh,
        in_specs=(P(None, "dp", None), P(None, "proto")),
        out_specs=(P(None, "dp", None), P("dp", "proto")),
        check_vma=False,
    )
```

```python
import jax
import jax.numpy as jnp
from jax import lax
from jax.experimental import pallas as pl
from jax.experimental.pallas import tpu as pltpu
from jax.sharding import PartitionSpec as P

MESH = pl.DeviceIdType.MESH
F32 = jnp.float32
BF16 = jnp.bfloat16

RING = 8
XS = 4
D = 256
COLS = 2048
HALF = 1024
CH = 256
ORDER = (4, 3, 5, 2, 6, 1, 7)


def place():
    dp = lax.axis_index("dp")
    x = lax.axis_index("proto")
    return lax.div(dp, 16), lax.rem(lax.div(dp, 2), RING), lax.rem(dp, 2), x


def device(y, z, c, x):
    return (y * 16 + z * 2 + c, x)


def kernel(
    emb_hbm,
    proto_ref,
    ge_ref,
    gp_ref,
    emb_ref,
    praw,
    pn,
    usend,
    urecv,
    uall,
    ut,
    e_ref,
    m_ref,
    cpart,
    csend,
    crecv,
    cvec,
    racc,
    rsend,
    rrecv,
    rb,
    zb,
    g_ref,
    gpart,
    rs_recv,
    p2send,
    p2recv,
    fin,
    fin_recv,
    gu_send,
    gu_recv,
    gx,
    gx_recv,
    gef,
    psem,
    ssem,
    rsem,
):
    y, z, c, x = place()
    used = [0]
    ends = []

    def sem():
        used[0] += 1
        return used[0] - 1

    def along(axis, s):
        if axis == "y":
            return device(lax.rem(y + s, RING), z, c, x)
        return device(y, lax.rem(z + s, RING), c, x)

    sibling = device(y, z, 1 - c, x)

    def remote(src, dst, k, target):
        return pltpu.make_async_remote_copy(
            src_ref=src,
            dst_ref=dst,
            send_sem=ssem.at[k],
            recv_sem=rsem.at[k],
            device_id=target,
            device_id_type=MESH,
        )

    def send(src, dst, target):
        k = sem()
        copy = remote(src, dst, k, target)
        copy.start()
        ends.append(copy.wait_send)
        return copy.wait_recv

    def fan(parts, whole):
        k = sem()
        for src, dst, target in parts:
            remote(src, dst, k, target).start()
        ends.append(lambda: pltpu.make_async_copy(whole, whole, ssem.at[k]).wait())
        return lambda: pltpu.make_async_copy(whole, whole, rsem.at[k]).wait()

    load_emb = pltpu.make_async_copy(emb_hbm, emb_ref, psem.at[0])
    load_emb.start()
    load = pltpu.make_async_copy(
        proto_ref.at[:, pl.ds(pl.multiple_of(c * COLS, COLS), COLS)], praw, psem.at[1]
    )
    load.start()

    row_peers = [(s // 2, s % 2) for s in range(1, 2 * XS)]

    def row_peer(dx, dc):
        return device(y, z, lax.rem(c + dc, 2), lax.rem(x + dx, XS))

    barrier = pltpu.get_barrier_semaphore()
    peers = [along("y", s) for s in ORDER] + [along("z", s) for s in ORDER]
    peers += [row_peer(*p) for p in row_peers]
    for target in peers:
        pl.semaphore_signal(barrier, inc=1, device_id=target, device_id_type=MESH)

    def unit_rows(i, carry):
        wide = emb_ref[i].astype(F32)
        inv = lax.rsqrt(jnp.mean(wide * wide, axis=-1, keepdims=True) + 1e-06)
        half = (wide * inv * 0.0625).astype(BF16)
        rows = pl.ds(pl.multiple_of(i * 64, 64), 64)
        usend[rows, :] = half.astype(F32)
        uall[c, rows, :] = half
        return carry

    load_emb.wait()
    lax.fori_loop(0, 4, unit_rows, 0)
    load.wait()

    def unit_protos(i, carry):
        cols = pl.ds(pl.multiple_of(i * 256, 256), 256)
        wide = praw[:, cols].astype(F32)
        inv = lax.rsqrt(jnp.mean(wide * wide, axis=0, keepdims=True) + 1e-06)
        pn[:, cols] = (wide * inv * 0.0625).astype(BF16)
        return carry

    lax.fori_loop(0, COLS // 256, unit_protos, 0)

    def scores(slot, first, lo, hi):
        def step(i, carry):
            cols = pl.ds(pl.multiple_of(i * 512, 512), 512)
            s = jnp.dot(uall[slot], pn[:, cols], preferred_element_type=F32)
            e = jnp.exp(s * 10.0)
            for v in range(2):
                part = e[v * 128 : (v + 1) * 128, :]
                e_ref[slot * 2 + v, :, cols] = part
                k = jnp.sum((part * part).reshape(16, 8, 512), axis=0)
                if first:
                    cpart[v, :, cols] = k
                else:
                    cpart[v, :, cols] += k
            return carry

        lax.fori_loop(lo, hi, step, 0)

    scores(c, True, 0, 2)
    pl.semaphore_wait(barrier, len(peers))
    got_u = send(usend, urecv, sibling)
    scores(c, True, 2, 4)
    got_u()
    uall[1 - c] = urecv[...].astype(BF16)

    def columns_start(it, h):
        for v in range(2):
            for t in range(8):
                col = h * HALF + t * 128
                csend[it, 0, h, v, t : t + 1, :] = jnp.sum(
                    cpart[v, :, col : col + 128], axis=0, keepdims=True
                )
        return columns_go(it, 0, h)

    def columns_go(it, ph, h):
        axis = "y" if (ph + h) % 2 == 0 else "z"
        return fan(
            [(csend.at[it, ph, h], crecv.at[it, ph, h, s - 1], along(axis, s)) for s in ORDER],
            crecv.at[it, ph, h],
        )

    def columns_sum(it, ph, h):
        total = csend[it, ph, h]
        for s in range(RING - 1):
            total = total + crecv[it, ph, h, s]
        return total

    def columns_next(it, h):
        csend[it, 1, h] = columns_sum(it, 0, h)
        return columns_go(it, 1, h)

    def columns_end(it, h):
        cvec[:, h * 8 : h * 8 + 8, :] = 1.0 / columns_sum(it, 1, h)

    def row_pass(it, h):
        def step(i, carry):
            q = lax.div(i, 2)
            v = lax.rem(q, 2)
            rows = pl.ds(pl.multiple_of(lax.rem(i, 2) * 64, 64), 64)
            if h == 0:
                acc = jnp.zeros((64, 128), F32)
                tot = jnp.zeros((64, 128), F32)
            else:
                acc = racc[0, q, rows, :]
                tot = racc[1, q, rows, :] if it == 0 else None
            for t in range(h * 8, h * 8 + 8):
                e = e_ref[q, rows, t * 128 : (t + 1) * 128]
                acc = acc + e * e * cvec[v, t : t + 1, :]
                if it == 0:
                    tot = tot + e
            racc[0, q, rows, :] = acc
            if it == 0:
                racc[1, q, rows, :] = tot
            return carry

        lax.fori_loop(0, 8, step, 0)

    def row_start(it):
        for w in range(2):
            for q in range(4):
                if it == 0 or w == 0:
                    row = jnp.sum(racc[w, q].T, axis=0, keepdims=True)
                else:
                    row = jnp.zeros((1, 128), F32)
                rsend[it, w * 4 + q : w * 4 + q + 1, :] = row
        return fan(
            [(rsend.at[it], rrecv.at[it, i], row_peer(*p)) for i, p in enumerate(row_peers)],
            rrecv.at[it],
        )

    def row_end(it):
        total = rsend[it]
        for i in range(len(row_peers)):
            total = total + rrecv[it, i]
        scale = 1.0 / total
        if it == 1:
            scale = scale * 10.0
        for q in range(4):
            rb[q] = jnp.broadcast_to(scale[q : q + 1, :], (128, 128)).T
            if it == 0:
                zb[q] = jnp.broadcast_to(scale[4 + q : 5 + q, :] * 10.0, (128, 128)).T

    def column_pass(h):
        def step(i, carry):
            v = lax.rem(i, 2)
            base = h * HALF + lax.div(i, 2) * 512
            acc = [jnp.zeros((8, 128), F32) for _ in range(4)]

            def rows32(j, acc):
                acc = list(acc)
                for slot in range(2):
                    for w in range(4):
                        rows = pl.ds(pl.multiple_of(j * 32 + w * 8, 8), 8)
                        r = rb[slot * 2 + v, rows, :]
                        for t in range(4):
                            cols = pl.ds(pl.multiple_of(base + t * 128, 128), 128)
                            e = e_ref[slot * 2 + v, rows, cols]
                            acc[t] = acc[t] + e * e * r
                return tuple(acc)

            acc = lax.fori_loop(0, 4, rows32, tuple(acc))
            for t in range(4):
                cols = pl.ds(pl.multiple_of(base + t * 128, 128), 128)
                cpart[v, :, cols] = acc[t]
            return carry

        lax.fori_loop(0, 4, step, 0)

    scores(1 - c, False, 0, 2)
    first_a = columns_start(0, 0)
    scores(1 - c, False, 2, 4)
    first_b = columns_start(0, 1)
    for it in range(2):
        first_a()
        second_a = columns_next(it, 0)
        first_b()
        second_b = columns_next(it, 1)
        second_a()
        columns_end(it, 0)
        row_pass(it, 0)
        second_b()
        columns_end(it, 1)
        row_pass(it, 1)
        got_rows = row_start(it)
        if it == 0:
            got_rows()
            row_end(it)
            column_pass(0)
            first_a = columns_start(1, 0)
            column_pass(1)
            first_b = columns_start(1, 1)

    def scaled(i, carry):
        q = lax.div(i, 4)
        v = lax.rem(q, 2)
        rows = pl.ds(pl.multiple_of(lax.rem(i, 4) * 32, 32), 32)
        zr = zb[q, rows, :]
        for t in range(COLS // 128):
            cols = slice(t * 128, (t + 1) * 128)
            e = e_ref[q, rows, cols]
            m_ref[q, rows, cols] = e * e * cvec[v, t : t + 1, :]
            e_ref[q, rows, cols] = e * zr
        return carry

    lax.fori_loop(0, 16, scaled, 0)

    to = lax.broadcasted_iota(jnp.int32, (D, D), 0)
    at = lax.broadcasted_iota(jnp.int32, (D, D), 1)
    natural = (to == at).astype(BF16)
    swapped = ((to // 32) * 4 + ((to // 4) % 8) * 32 + to % 4 == at).astype(BF16)
    for h, order in ((0, natural), (1, swapped)):
        for slot in range(2):
            ut[h, :, slot * 256 : (slot + 1) * 256] = lax.dot_general(
                order, uall[slot], (((1,), (1,)), ((), ())), preferred_element_type=F32
            ).astype(BF16)

    got_rows()
    row_end(1)

    chunks = []
    for j in range(HALF // CH):
        sign = 1 if j % 2 == 0 else -1
        chunks.append(("y", "z", 0, j * CH, sign))
        chunks.append(("z", "y", 1, HALF + j * CH, sign))
    own = {"y": y, "z": z}

    def slab(ch, s):
        which = lax.rem(own[chunks[ch][0]] + (s + RING), RING)
        return gpart.at[ch, pl.ds(pl.multiple_of(which * 32, 32), 32), :]

    flight = {}

    def hop(ch, way, src, s):
        flight[ch, way] = send(src, rs_recv.at[ch, way], along(chunks[ch][0], s % RING))

    def step0(ch):
        sign = chunks[ch][4]
        hop(ch, 6, slab(ch, 4 * sign), 2 * sign)
        hop(ch, 0, slab(ch, 3 * sign), sign)
        hop(ch, 3, slab(ch, -3 * sign), -sign)

    def step1(ch):
        sign = chunks[ch][4]
        flight[ch, 3]()
        here = rs_recv.at[ch, 3]
        here[...] = here[...] + slab(ch, -2 * sign)[...]
        hop(ch, 4, here, -sign)
        flight[ch, 0]()
        flight[ch, 6]()
        here = rs_recv.at[ch, 0]
        here[...] = here[...] + rs_recv[ch, 6] + slab(ch, 2 * sign)[...]
        hop(ch, 1, here, sign)

    def step2(ch):
        for way, sign in ((1, chunks[ch][4]), (4, -chunks[ch][4])):
            flight[ch, way]()
            here = rs_recv.at[ch, way]
            here[...] = here[...] + slab(ch, sign)[...]
            hop(ch, way + 1, here, sign)

    got_p2 = {}

    def step3(ch):
        axis2 = chunks[ch][1]
        flight[ch, 2]()
        flight[ch, 5]()
        total = slab(ch, 0)[...] + rs_recv[ch, 2] + rs_recv[ch, 5]
        for q in range(RING):
            p2send[ch, q] = total[q * 4 : q * 4 + 4, :]
        got_p2[ch] = fan(
            [
                (p2send.at[ch, lax.rem(own[axis2] + s, RING)], p2recv.at[ch, s - 1], along(axis2, s))
                for s in ORDER
            ],
            p2recv.at[ch],
        )

    for ch, (_, _, h, col0, _) in enumerate(chunks):
        def terms(i, carry):
            slot = lax.div(i, 2)
            for v in range(2):
                q = slot * 2 + v
                o = slot * 2 + 1 - v
                for w in range(2):
                    row0 = lax.rem(i, 2) * 64 + w * 32
                    rows = pl.ds(pl.multiple_of(row0, 32), 32)
                    r = rb[o, rows, :]
                    to_rows = pl.ds(pl.multiple_of(q * 128 + row0, 32), 32)
                    for t in range(CH // 128):
                        cols = slice(col0 + t * 128, col0 + (t + 1) * 128)
                        g_ref[to_rows, cols] = (
                            e_ref[q, rows, cols] - m_ref[o, rows, cols] * r
                        ).astype(BF16)
            return carry

        lax.fori_loop(0, 4, terms, 0)
        gpart[ch] = jnp.dot(ut[h], g_ref[:, col0 : col0 + CH], preferred_element_type=F32)
        step0(ch)

    def back(slot):
        return lax.dot_general(
            g_ref[pl.ds(pl.multiple_of(slot * 256, 256), 256), :],
            pn[...],
            (((1,), (1,)), ((), ())),
            preferred_element_type=F32,
        )

    def along_x(s):
        return device(y, z, c, lax.rem(x + s, XS))

    gu_send[...] = back(1 - c)
    got_gu = send(gu_send, gu_recv, sibling)
    gx[...] = back(c).reshape(4, 64, 256)
    for ch in range(len(chunks) // 2):
        step1(ch)
    got_gu()
    gx[...] = gx[...] + gu_recv[...].reshape(4, 64, 256)
    got_gx = fan(
        [(gx.at[lax.rem(x + s, XS)], gx_recv.at[s - 1], along_x(s)) for s in (2, 1, 3)], gx_recv
    )
    for ch in range(len(chunks) // 2, len(chunks)):
        step1(ch)
    for ch in range(len(chunks)):
        step2(ch)
    for ch in range(len(chunks) // 2):
        step3(ch)

    got_gx()
    g = gx[x] + gx_recv[0] + gx_recv[1] + gx_recv[2]
    wide = emb_ref[x].astype(F32)
    inv = lax.rsqrt(jnp.mean(wide * wide, axis=-1, keepdims=True) + 1e-06)
    mean = jnp.mean(wide * g, axis=-1, keepdims=True)
    gef[x] = (g * inv - wide * (inv * inv * inv * mean)) * 0.0625
    got_ge = [send(gef.at[x], gef.at[x], along_x(s)) for s in (2, 1, 3)]

    for ch in range(len(chunks) // 2, len(chunks)):
        step3(ch)

    def second(ch):
        _, axis2, _, col0, _ = chunks[ch]
        got_p2[ch]()
        total = p2send[ch, own[axis2]]
        for s in range(RING - 1):
            total = total + p2recv[ch, s]
        for q in range(2):
            fin[q, :, col0 : col0 + CH] = total[q * 2 : q * 2 + 2, :]

    for ch in range(len(chunks)):
        second(ch)
    got_fin = send(fin.at[1 - c], fin_recv, sibling)
    gp_ref[:, pl.ds(pl.multiple_of(c * COLS, COLS), COLS)] = fin[c]
    for wait in got_ge:
        wait()
    ge_ref[...] = gef[...]
    got_fin()
    gp_ref[:, pl.ds(pl.multiple_of((1 - c) * COLS, COLS), COLS)] = fin_recv[...]

    for wait in ends:
        wait()
    assert used[0] <= SEMS


SEMS = 96


def shards(embeddings, prototypes):
    vmem = pl.BlockSpec(memory_space=pltpu.VMEM)
    ge, gp = pl.pallas_call(
        kernel,
        name="swap_step",
        out_shape=(
            jax.ShapeDtypeStruct((4, 64, D), F32),
            jax.ShapeDtypeStruct((2, 2 * COLS), F32),
        ),
        in_specs=[pl.BlockSpec(memory_space=pltpu.HBM)] * 2,
        out_specs=(vmem, vmem),
        scratch_shapes=[
            pltpu.VMEM((4, 64, D), BF16),
            pltpu.VMEM((D, COLS), BF16),
            pltpu.VMEM((D, COLS), BF16),
            pltpu.VMEM((256, D), F32),
            pltpu.VMEM((256, D), F32),
            pltpu.VMEM((2, 256, D), BF16),
            pltpu.VMEM((2, D, 512), BF16),
            pltpu.VMEM((4, 128, COLS), F32),
            pltpu.VMEM((4, 128, COLS), F32),
            pltpu.VMEM((2, 8, COLS), F32),
            pltpu.VMEM((2, 2, 2, 2, 8, 128), F32),
            pltpu.VMEM((2, 2, 2, RING - 1, 2, 8, 128), F32),
            pltpu.VMEM((2, 16, 128), F32),
            pltpu.VMEM((2, 4, 128, 128), F32),
            pltpu.VMEM((2, 8, 128), F32),
            pltpu.VMEM((2, 2 * XS - 1, 8, 128), F32),
            pltpu.VMEM((4, 128, 128), F32),
            pltpu.VMEM((4, 128, 128), F32),
            pltpu.VMEM((512, COLS), BF16),
            pltpu.VMEM((8, D, CH), F32),
            pltpu.VMEM((8, 7, 32, CH), F32),
            pltpu.VMEM((8, RING, 4, CH), F32),
            pltpu.VMEM((8, RING - 1, 4, CH), F32),
            pltpu.VMEM((2, 2, COLS), F32),
            pltpu.VMEM((2, COLS), F32),
            pltpu.VMEM((256, D), F32),
            pltpu.VMEM((256, D), F32),
            pltpu.VMEM((4, 64, D), F32),
            pltpu.VMEM((3, 64, D), F32),
            pltpu.VMEM((4, 64, D), F32),
            pltpu.SemaphoreType.DMA((2,)),
            pltpu.SemaphoreType.DMA((SEMS,)),
            pltpu.SemaphoreType.DMA((SEMS,)),
        ],
        compiler_params=pltpu.CompilerParams(
            collective_id=0, has_side_effects=True, vmem_limit_bytes=52 << 20
        ),
        cost_estimate=pl.CostEstimate(
            flops=2_000_000_000, bytes_accessed=4_000_000, transcendentals=1_100_000
        ),
    )(embeddings.reshape(4, 64, D), prototypes)
    return ge.reshape(2, 128, D), gp


def solution(mesh):
    return jax.shard_map(
        shards,
        mesh=mesh,
        in_specs=(P(None, "dp", None), P(None, "proto")),
        out_specs=(P(None, "dp", None), P("dp", "proto")),
        check_vma=False,
    )
```

```python
import jax
import jax.numpy as jnp
from jax import lax
from jax.experimental import pallas as pl
from jax.experimental.pallas import tpu as pltpu
from jax.sharding import PartitionSpec as P

MESH = pl.DeviceIdType.MESH
F32 = jnp.float32
BF16 = jnp.bfloat16

RING = 8
XS = 4
D = 256
COLS = 2048
HALF = 1024
CH = 256
CHUNKS = COLS // CH
ORDER = (4, 3, 5, 2, 6, 1, 7)


def place():
    dp = lax.axis_index("dp")
    x = lax.axis_index("proto")
    return lax.div(dp, 16), lax.rem(lax.div(dp, 2), RING), lax.rem(dp, 2), x


def device(y, z, c, x):
    return (y * 16 + z * 2 + c, x)


def kernel(
    emb_hbm,
    proto_ref,
    ge_ref,
    gp_ref,
    emb_ref,
    praw,
    pn,
    usend,
    urecv,
    uall,
    ut,
    e_ref,
    m_ref,
    cpart,
    csend,
    crecv,
    cvec,
    racc,
    rsend,
    rrecv,
    rb,
    zb,
    g_ref,
    gpart,
    rs_recv,
    p2send,
    p2recv,
    fin,
    fin_recv,
    gu_send,
    gu_recv,
    gx,
    gx_recv,
    gef,
    psem,
    ssem,
    rsem,
):
    y, z, c, x = place()
    used = [0]
    ends = []

    def sem():
        used[0] += 1
        return used[0] - 1

    def along(axis, s):
        if axis == "y":
            return device(lax.rem(y + s, RING), z, c, x)
        return device(y, lax.rem(z + s, RING), c, x)

    sibling = device(y, z, 1 - c, x)

    def remote(src, dst, k, target):
        return pltpu.make_async_remote_copy(
            src_ref=src,
            dst_ref=dst,
            send_sem=ssem.at[k],
            recv_sem=rsem.at[k],
            device_id=target,
            device_id_type=MESH,
        )

    def send(src, dst, target):
        k = sem()
        copy = remote(src, dst, k, target)
        copy.start()
        ends.append(copy.wait_send)
        return copy.wait_recv

    def fan(parts, whole):
        k = sem()
        for src, dst, target in parts:
            remote(src, dst, k, target).start()
        ends.append(lambda: pltpu.make_async_copy(whole, whole, ssem.at[k]).wait())
        return lambda: pltpu.make_async_copy(whole, whole, rsem.at[k]).wait()

    load_emb = pltpu.make_async_copy(emb_hbm, emb_ref, psem.at[0])
    load_emb.start()
    load = pltpu.make_async_copy(
        proto_ref.at[:, pl.ds(pl.multiple_of(c * COLS, COLS), COLS)], praw, psem.at[1]
    )
    load.start()

    row_peers = [(s // 2, s % 2) for s in range(1, 2 * XS)]

    def row_peer(dx, dc):
        return device(y, z, lax.rem(c + dc, 2), lax.rem(x + dx, XS))

    barrier = pltpu.get_barrier_semaphore()
    peers = [along("y", s) for s in ORDER] + [along("z", s) for s in ORDER]
    peers += [row_peer(*p) for p in row_peers]
    for target in peers:
        pl.semaphore_signal(barrier, inc=1, device_id=target, device_id_type=MESH)

    def unit_rows(i, carry):
        wide = emb_ref[i].astype(F32)
        inv = lax.rsqrt(jnp.mean(wide * wide, axis=-1, keepdims=True) + 1e-06)
        half = (wide * inv * 0.0625).astype(BF16)
        rows = pl.ds(pl.multiple_of(i * 64, 64), 64)
        usend[rows, :] = half.astype(F32)
        uall[c, rows, :] = half
        return carry

    load_emb.wait()
    lax.fori_loop(0, 4, unit_rows, 0)
    load.wait()

    def unit_protos(i, carry):
        cols = pl.ds(pl.multiple_of(i * 256, 256), 256)
        wide = praw[:, cols].astype(F32)
        inv = lax.rsqrt(jnp.mean(wide * wide, axis=0, keepdims=True) + 1e-06)
        pn[:, cols] = (wide * inv * 0.0625).astype(BF16)
        return carry

    lax.fori_loop(0, COLS // 256, unit_protos, 0)

    def scores(slot, first, lo, hi):
        def step(i, carry):
            cols = pl.ds(pl.multiple_of(i * 512, 512), 512)
            s = jnp.dot(uall[slot], pn[:, cols], preferred_element_type=F32)
            e = jnp.exp(s * 10.0)
            for v in range(2):
                part = e[v * 128 : (v + 1) * 128, :]
                e_ref[slot * 2 + v, :, cols] = part
                k = jnp.sum((part * part).reshape(16, 8, 512), axis=0)
                if first:
                    cpart[v, :, cols] = k
                else:
                    cpart[v, :, cols] += k
            return carry

        lax.fori_loop(lo, hi, step, 0)

    scores(c, True, 0, 2)
    pl.semaphore_wait(barrier, len(peers))
    got_u = send(usend, urecv, sibling)
    scores(c, True, 2, 4)
    got_u()
    uall[1 - c] = urecv[...].astype(BF16)

    def columns_start(it, h):
        for v in range(2):
            for t in range(8):
                col = h * HALF + t * 128
                csend[it, 0, h, v, t : t + 1, :] = jnp.sum(
                    cpart[v, :, col : col + 128], axis=0, keepdims=True
                )
        return columns_go(it, 0, h)

    def columns_go(it, ph, h):
        axis = "y" if (ph + h) % 2 == 0 else "z"
        return fan(
            [(csend.at[it, ph, h], crecv.at[it, ph, h, s - 1], along(axis, s)) for s in ORDER],
            crecv.at[it, ph, h],
        )

    def columns_sum(it, ph, h):
        total = csend[it, ph, h]
        for s in range(RING - 1):
            total = total + crecv[it, ph, h, s]
        return total

    def columns_next(it, h):
        csend[it, 1, h] = columns_sum(it, 0, h)
        return columns_go(it, 1, h)

    def columns_end(it, h):
        cvec[:, h * 8 : h * 8 + 8, :] = 1.0 / columns_sum(it, 1, h)

    def row_pass(it, h):
        def step(i, carry):
            q = lax.div(i, 2)
            v = lax.rem(q, 2)
            rows = pl.ds(pl.multiple_of(lax.rem(i, 2) * 64, 64), 64)
            if h == 0:
                acc = jnp.zeros((64, 128), F32)
                tot = jnp.zeros((64, 128), F32)
            else:
                acc = racc[0, q, rows, :]
                tot = racc[1, q, rows, :] if it == 0 else None
            for t in range(h * 8, h * 8 + 8):
                e = e_ref[q, rows, t * 128 : (t + 1) * 128]
                acc = acc + e * e * cvec[v, t : t + 1, :]
                if it == 0:
                    tot = tot + e
            racc[0, q, rows, :] = acc
            if it == 0:
                racc[1, q, rows, :] = tot
            return carry

        lax.fori_loop(0, 8, step, 0)

    def row_start(it):
        for w in range(2):
            for q in range(4):
                if it == 0 or w == 0:
                    row = jnp.sum(racc[w, q].T, axis=0, keepdims=True)
                else:
                    row = jnp.zeros((1, 128), F32)
                rsend[it, w * 4 + q : w * 4 + q + 1, :] = row
        return fan(
            [(rsend.at[it], rrecv.at[it, i], row_peer(*p)) for i, p in enumerate(row_peers)],
            rrecv.at[it],
        )

    def row_end(it):
        total = rsend[it]
        for i in range(len(row_peers)):
            total = total + rrecv[it, i]
        scale = 1.0 / total
        if it == 1:
            scale = scale * 10.0
        for q in range(4):
            rb[q] = jnp.broadcast_to(scale[q : q + 1, :], (128, 128)).T
            if it == 0:
                zb[q] = jnp.broadcast_to(scale[4 + q : 5 + q, :] * 10.0, (128, 128)).T

    def column_pass(h):
        def step(i, carry):
            v = lax.rem(i, 2)
            base = h * HALF + lax.div(i, 2) * 512
            acc = [jnp.zeros((8, 128), F32) for _ in range(4)]

            def rows32(j, acc):
                acc = list(acc)
                for slot in range(2):
                    for w in range(4):
                        rows = pl.ds(pl.multiple_of(j * 32 + w * 8, 8), 8)
                        r = rb[slot * 2 + v, rows, :]
                        for t in range(4):
                            cols = pl.ds(pl.multiple_of(base + t * 128, 128), 128)
                            e = e_ref[slot * 2 + v, rows, cols]
                            acc[t] = acc[t] + e * e * r
                return tuple(acc)

            acc = lax.fori_loop(0, 4, rows32, tuple(acc))
            for t in range(4):
                cols = pl.ds(pl.multiple_of(base + t * 128, 128), 128)
                cpart[v, :, cols] = acc[t]
            return carry

        lax.fori_loop(0, 4, step, 0)

    scores(1 - c, False, 0, 2)
    first_a = columns_start(0, 0)
    scores(1 - c, False, 2, 4)
    first_b = columns_start(0, 1)
    for it in range(2):
        first_a()
        second_a = columns_next(it, 0)
        first_b()
        second_b = columns_next(it, 1)
        second_a()
        columns_end(it, 0)
        row_pass(it, 0)
        second_b()
        columns_end(it, 1)
        row_pass(it, 1)
        got_rows = row_start(it)
        if it == 0:
            got_rows()
            row_end(it)
            column_pass(0)
            first_a = columns_start(1, 0)
            column_pass(1)
            first_b = columns_start(1, 1)

    def scaled(i, carry):
        q = lax.div(i, 4)
        v = lax.rem(q, 2)
        rows = pl.ds(pl.multiple_of(lax.rem(i, 4) * 32, 32), 32)
        zr = zb[q, rows, :]
        for t in range(COLS // 128):
            cols = slice(t * 128, (t + 1) * 128)
            e = e_ref[q, rows, cols]
            m_ref[q, rows, cols] = e * e * cvec[v, t : t + 1, :]
            e_ref[q, rows, cols] = e * zr
        return carry

    lax.fori_loop(0, 16, scaled, 0)

    to = lax.broadcasted_iota(jnp.int32, (D, D), 0)
    at = lax.broadcasted_iota(jnp.int32, (D, D), 1)
    natural = (to == at).astype(BF16)
    swapped = ((to // 32) * 4 + ((to // 4) % 8) * 32 + to % 4 == at).astype(BF16)
    for h, order in ((0, natural), (1, swapped)):
        for slot in range(2):
            ut[h, :, slot * 256 : (slot + 1) * 256] = lax.dot_general(
                order, uall[slot], (((1,), (1,)), ((), ())), preferred_element_type=F32
            ).astype(BF16)

    got_rows()
    row_end(1)

    chunks = []
    for j in range(HALF // CH):
        sign = 1 if j % 2 == 0 else -1
        chunks.append(("y", "z", 0, j * CH, sign))
        chunks.append(("z", "y", 1, HALF + j * CH, sign))
    own = {"y": y, "z": z}

    def slab(ch, s):
        which = lax.rem(own[chunks[ch][0]] + (s + RING), RING)
        return gpart.at[ch, pl.ds(pl.multiple_of(which * 32, 32), 32), :]

    flight = {}

    def hop(ch, way, src, s):
        flight[ch, way] = send(src, rs_recv.at[ch, way], along(chunks[ch][0], s % RING))

    def step0(ch):
        sign = chunks[ch][4]
        hop(ch, 6, slab(ch, 4 * sign), 2 * sign)
        hop(ch, 0, slab(ch, 3 * sign), sign)
        hop(ch, 3, slab(ch, -3 * sign), -sign)

    def step1(ch):
        sign = chunks[ch][4]
        flight[ch, 3]()
        here = rs_recv.at[ch, 3]
        here[...] = here[...] + slab(ch, -2 * sign)[...]
        hop(ch, 4, here, -sign)
        flight[ch, 0]()
        flight[ch, 6]()
        here = rs_recv.at[ch, 0]
        here[...] = here[...] + rs_recv[ch, 6] + slab(ch, 2 * sign)[...]
        hop(ch, 1, here, sign)

    def step2(ch):
        for way, sign in ((1, chunks[ch][4]), (4, -chunks[ch][4])):
            flight[ch, way]()
            here = rs_recv.at[ch, way]
            here[...] = here[...] + slab(ch, sign)[...]
            hop(ch, way + 1, here, sign)

    got_p2 = {}

    def step3(ch):
        axis2 = chunks[ch][1]
        flight[ch, 2]()
        flight[ch, 5]()
        total = slab(ch, 0)[...] + rs_recv[ch, 2] + rs_recv[ch, 5]
        for q in range(RING):
            p2send[ch, q] = total[q * 4 : q * 4 + 4, :]
        got_p2[ch] = fan(
            [
                (p2send.at[ch, lax.rem(own[axis2] + s, RING)], p2recv.at[ch, s - 1], along(axis2, s))
                for s in ORDER
            ],
            p2recv.at[ch],
        )

    def terms(ch):
        for q in range(4):
            o = q + 1 - 2 * (q % 2)
            for t in range(CH // 128):
                cols = slice(chunks[ch][3] + t * 128, chunks[ch][3] + (t + 1) * 128)
                g_ref[q * 128 : (q + 1) * 128, cols] = (
                    e_ref[q, :, cols] - m_ref[o, :, cols] * rb[o]
                ).astype(BF16)

    terms(0)
    for ch, (_, _, h, col0, _) in enumerate(chunks):
        if ch + 1 < len(chunks):
            terms(ch + 1)
        gpart[ch] = jnp.dot(ut[h], g_ref[:, col0 : col0 + CH], preferred_element_type=F32)
        step0(ch)

    def back(slot):
        return lax.dot_general(
            g_ref[pl.ds(pl.multiple_of(slot * 256, 256), 256), :],
            pn[...],
            (((1,), (1,)), ((), ())),
            preferred_element_type=F32,
        )

    def along_x(s):
        return device(y, z, c, lax.rem(x + s, XS))

    gu_send[...] = back(1 - c)
    got_gu = send(gu_send, gu_recv, sibling)
    gx[...] = back(c).reshape(4, 64, 256)
    for ch in range(len(chunks) // 2):
        step1(ch)
    got_gu()
    gx[...] = gx[...] + gu_recv[...].reshape(4, 64, 256)
    got_gx = fan(
        [(gx.at[lax.rem(x + s, XS)], gx_recv.at[s - 1], along_x(s)) for s in (2, 1, 3)], gx_recv
    )
    for ch in range(len(chunks) // 2, len(chunks)):
        step1(ch)
    for ch in range(len(chunks)):
        step2(ch)
    for ch in range(len(chunks) // 2):
        step3(ch)

    got_gx()
    g = gx[x] + gx_recv[0] + gx_recv[1] + gx_recv[2]
    wide = emb_ref[x].astype(F32)
    inv = lax.rsqrt(jnp.mean(wide * wide, axis=-1, keepdims=True) + 1e-06)
    mean = jnp.mean(wide * g, axis=-1, keepdims=True)
    gef[x] = (g * inv - wide * (inv * inv * inv * mean)) * 0.0625
    got_ge = [send(gef.at[x], gef.at[x], along_x(s)) for s in (2, 1, 3)]

    for ch in range(len(chunks) // 2, len(chunks)):
        step3(ch)

    def second(ch):
        _, axis2, _, col0, _ = chunks[ch]
        got_p2[ch]()
        total = p2send[ch, own[axis2]]
        for s in range(RING - 1):
            total = total + p2recv[ch, s]
        for q in range(2):
            fin[q, :, col0 : col0 + CH] = total[q * 2 : q * 2 + 2, :]

    for ch in range(len(chunks)):
        second(ch)
    got_fin = send(fin.at[1 - c], fin_recv, sibling)
    gp_ref[:, pl.ds(pl.multiple_of(c * COLS, COLS), COLS)] = fin[c]
    for wait in got_ge:
        wait()
    ge_ref[...] = gef[...]
    got_fin()
    gp_ref[:, pl.ds(pl.multiple_of((1 - c) * COLS, COLS), COLS)] = fin_recv[...]

    for wait in ends:
        wait()
    assert used[0] <= SEMS


SEMS = 96


def shards(embeddings, prototypes):
    vmem = pl.BlockSpec(memory_space=pltpu.VMEM)
    ge, gp = pl.pallas_call(
        kernel,
        name="swap_step",
        out_shape=(
            jax.ShapeDtypeStruct((4, 64, D), F32),
            jax.ShapeDtypeStruct((2, 2 * COLS), F32),
        ),
        in_specs=[pl.BlockSpec(memory_space=pltpu.HBM)] * 2,
        out_specs=(vmem, vmem),
        scratch_shapes=[
            pltpu.VMEM((4, 64, D), BF16),
            pltpu.VMEM((D, COLS), BF16),
            pltpu.VMEM((D, COLS), BF16),
            pltpu.VMEM((256, D), F32),
            pltpu.VMEM((256, D), F32),
            pltpu.VMEM((2, 256, D), BF16),
            pltpu.VMEM((2, D, 512), BF16),
            pltpu.VMEM((4, 128, COLS), F32),
            pltpu.VMEM((4, 128, COLS), F32),
            pltpu.VMEM((2, 8, COLS), F32),
            pltpu.VMEM((2, 2, 2, 2, 8, 128), F32),
            pltpu.VMEM((2, 2, 2, RING - 1, 2, 8, 128), F32),
            pltpu.VMEM((2, 16, 128), F32),
            pltpu.VMEM((2, 4, 128, 128), F32),
            pltpu.VMEM((2, 8, 128), F32),
            pltpu.VMEM((2, 2 * XS - 1, 8, 128), F32),
            pltpu.VMEM((4, 128, 128), F32),
            pltpu.VMEM((4, 128, 128), F32),
            pltpu.VMEM((512, COLS), BF16),
            pltpu.VMEM((CHUNKS, D, CH), F32),
            pltpu.VMEM((CHUNKS, 7, 32, CH), F32),
            pltpu.VMEM((CHUNKS, RING, 4, CH), F32),
            pltpu.VMEM((CHUNKS, RING - 1, 4, CH), F32),
            pltpu.VMEM((2, 2, COLS), F32),
            pltpu.VMEM((2, COLS), F32),
            pltpu.VMEM((256, D), F32),
            pltpu.VMEM((256, D), F32),
            pltpu.VMEM((4, 64, D), F32),
            pltpu.VMEM((3, 64, D), F32),
            pltpu.VMEM((4, 64, D), F32),
            pltpu.SemaphoreType.DMA((2,)),
            pltpu.SemaphoreType.DMA((SEMS,)),
            pltpu.SemaphoreType.DMA((SEMS,)),
        ],
        compiler_params=pltpu.CompilerParams(
            collective_id=0, has_side_effects=True, vmem_limit_bytes=52 << 20
        ),
        cost_estimate=pl.CostEstimate(
            flops=2_000_000_000, bytes_accessed=4_000_000, transcendentals=1_100_000
        ),
    )(embeddings.reshape(4, 64, D), prototypes)
    return ge.reshape(2, 128, D), gp


def solution(mesh):
    return jax.shard_map(
        shards,
        mesh=mesh,
        in_specs=(P(None, "dp", None), P(None, "proto")),
        out_specs=(P(None, "dp", None), P("dp", "proto")),
        check_vma=False,
    )
```

```python
import jax
import jax.numpy as jnp
from jax import lax
from jax.experimental import pallas as pl
from jax.experimental.pallas import tpu as pltpu
from jax.sharding import PartitionSpec as P

MESH = pl.DeviceIdType.MESH
F32 = jnp.float32
BF16 = jnp.bfloat16

RING = 8
XS = 4
D = 256
COLS = 2048
HALF = 1024
CH = 256
CHUNKS = COLS // CH
ORDER = (4, 3, 5, 2, 6, 1, 7)


def place():
    dp = lax.axis_index("dp")
    x = lax.axis_index("proto")
    return lax.div(dp, 16), lax.rem(lax.div(dp, 2), RING), lax.rem(dp, 2), x


def device(y, z, c, x):
    return (y * 16 + z * 2 + c, x)


def kernel(
    emb_hbm,
    proto_ref,
    ge_ref,
    gp_ref,
    emb_ref,
    praw,
    pn,
    usend,
    urecv,
    uall,
    ut,
    e_ref,
    m_ref,
    cpart,
    csend,
    crecv,
    cvec,
    racc,
    rsend,
    rrecv,
    rb,
    zb,
    g_ref,
    gpart,
    rs_recv,
    p2send,
    p2recv,
    fin,
    fin_recv,
    gu_send,
    gu_recv,
    gx,
    gx_recv,
    gef,
    psem,
    ssem,
    rsem,
):
    y, z, c, x = place()
    used = [0]
    ends = []

    def sem():
        used[0] += 1
        return used[0] - 1

    def along(axis, s):
        if axis == "y":
            return device(lax.rem(y + s, RING), z, c, x)
        return device(y, lax.rem(z + s, RING), c, x)

    sibling = device(y, z, 1 - c, x)

    def remote(src, dst, k, target):
        return pltpu.make_async_remote_copy(
            src_ref=src,
            dst_ref=dst,
            send_sem=ssem.at[k],
            recv_sem=rsem.at[k],
            device_id=target,
            device_id_type=MESH,
        )

    def send(src, dst, target):
        k = sem()
        copy = remote(src, dst, k, target)
        copy.start()
        ends.append(copy.wait_send)
        return copy.wait_recv

    def fan(parts, whole):
        k = sem()
        for src, dst, target in parts:
            remote(src, dst, k, target).start()
        ends.append(lambda: pltpu.make_async_copy(whole, whole, ssem.at[k]).wait())
        return lambda: pltpu.make_async_copy(whole, whole, rsem.at[k]).wait()

    load_emb = pltpu.make_async_copy(emb_hbm, emb_ref, psem.at[0])
    load_emb.start()
    load = pltpu.make_async_copy(
        proto_ref.at[:, pl.ds(pl.multiple_of(c * COLS, COLS), COLS)], praw, psem.at[1]
    )
    load.start()

    row_peers = [(2, 1), (2, 0), (1, 1), (3, 1), (1, 0), (3, 0), (0, 1)]

    def row_peer(dx, dc):
        return device(y, z, lax.rem(c + dc, 2), lax.rem(x + dx, XS))

    barrier = pltpu.get_barrier_semaphore()
    peers = [along("y", s) for s in ORDER] + [along("z", s) for s in ORDER]
    peers += [row_peer(*p) for p in row_peers]
    for target in peers:
        pl.semaphore_signal(barrier, inc=1, device_id=target, device_id_type=MESH)

    def unit_rows(i, carry):
        wide = emb_ref[i].astype(F32)
        inv = lax.rsqrt(jnp.mean(wide * wide, axis=-1, keepdims=True) + 1e-06)
        half = (wide * inv * 0.0625).astype(BF16)
        rows = pl.ds(pl.multiple_of(i * 64, 64), 64)
        usend[rows, :] = half.astype(F32)
        uall[c, rows, :] = half
        return carry

    load_emb.wait()
    lax.fori_loop(0, 4, unit_rows, 0)
    load.wait()

    def unit_protos(i, carry):
        cols = pl.ds(pl.multiple_of(i * 256, 256), 256)
        wide = praw[:, cols].astype(F32)
        inv = lax.rsqrt(jnp.mean(wide * wide, axis=0, keepdims=True) + 1e-06)
        pn[:, cols] = (wide * inv * 0.0625).astype(BF16)
        return carry

    lax.fori_loop(0, COLS // 256, unit_protos, 0)

    def scores(slot, first, lo, hi):
        def step(i, carry):
            cols = pl.ds(pl.multiple_of(i * 512, 512), 512)
            s = jnp.dot(uall[slot], pn[:, cols], preferred_element_type=F32)
            e = jnp.exp(s * 10.0)
            for v in range(2):
                part = e[v * 128 : (v + 1) * 128, :]
                e_ref[slot * 2 + v, :, cols] = part
                k = jnp.sum((part * part).reshape(16, 8, 512), axis=0)
                if first:
                    cpart[v, :, cols] = k
                else:
                    cpart[v, :, cols] += k
            return carry

        lax.fori_loop(lo, hi, step, 0)

    scores(c, True, 0, 2)
    pl.semaphore_wait(barrier, len(peers))
    got_u = send(usend, urecv, sibling)
    scores(c, True, 2, 4)
    got_u()
    uall[1 - c] = urecv[...].astype(BF16)

    def columns_start(it, h):
        for v in range(2):
            for t in range(8):
                col = h * HALF + t * 128
                csend[it, 0, h, v, t : t + 1, :] = jnp.sum(
                    cpart[v, :, col : col + 128], axis=0, keepdims=True
                )
        return columns_go(it, 0, h)

    def columns_go(it, ph, h):
        axis = "y" if (ph + h) % 2 == 0 else "z"
        return fan(
            [(csend.at[it, ph, h], crecv.at[it, ph, h, s - 1], along(axis, s)) for s in ORDER],
            crecv.at[it, ph, h],
        )

    def columns_sum(it, ph, h):
        total = csend[it, ph, h]
        for s in range(RING - 1):
            total = total + crecv[it, ph, h, s]
        return total

    def columns_next(it, h):
        csend[it, 1, h] = columns_sum(it, 0, h)
        return columns_go(it, 1, h)

    def columns_end(it, h):
        cvec[:, h * 8 : h * 8 + 8, :] = 1.0 / columns_sum(it, 1, h)

    def row_pass(it, h):
        def step(i, carry):
            q = lax.div(i, 2)
            v = lax.rem(q, 2)
            rows = pl.ds(pl.multiple_of(lax.rem(i, 2) * 64, 64), 64)
            if h == 0:
                acc = jnp.zeros((64, 128), F32)
                tot = jnp.zeros((64, 128), F32)
            else:
                acc = racc[0, q, rows, :]
                tot = racc[1, q, rows, :] if it == 0 else None
            for t in range(h * 8, h * 8 + 8):
                e = e_ref[q, rows, t * 128 : (t + 1) * 128]
                acc = acc + e * e * cvec[v, t : t + 1, :]
                if it == 0:
                    tot = tot + e
            racc[0, q, rows, :] = acc
            if it == 0:
                racc[1, q, rows, :] = tot
            return carry

        lax.fori_loop(0, 8, step, 0)

    def row_start(it):
        for w in range(2):
            for q in range(4):
                if it == 0 or w == 0:
                    row = jnp.sum(racc[w, q].T, axis=0, keepdims=True)
                else:
                    row = jnp.zeros((1, 128), F32)
                rsend[it, w * 4 + q : w * 4 + q + 1, :] = row
        return fan(
            [(rsend.at[it], rrecv.at[it, i], row_peer(*p)) for i, p in enumerate(row_peers)],
            rrecv.at[it],
        )

    def row_end(it):
        total = rsend[it]
        for i in range(len(row_peers)):
            total = total + rrecv[it, i]
        scale = 1.0 / total
        if it == 1:
            scale = scale * 10.0
        for q in range(4):
            rb[q] = jnp.broadcast_to(scale[q : q + 1, :], (128, 128)).T
            if it == 0:
                zb[q] = jnp.broadcast_to(scale[4 + q : 5 + q, :] * 10.0, (128, 128)).T

    def column_pass(h):
        def step(i, carry):
            v = lax.rem(i, 2)
            base = h * HALF + lax.div(i, 2) * 512
            acc = [jnp.zeros((8, 128), F32) for _ in range(4)]

            def rows32(j, acc):
                acc = list(acc)
                for slot in range(2):
                    for w in range(4):
                        rows = pl.ds(pl.multiple_of(j * 32 + w * 8, 8), 8)
                        r = rb[slot * 2 + v, rows, :]
                        for t in range(4):
                            cols = pl.ds(pl.multiple_of(base + t * 128, 128), 128)
                            e = e_ref[slot * 2 + v, rows, cols]
                            acc[t] = acc[t] + e * e * r
                return tuple(acc)

            acc = lax.fori_loop(0, 4, rows32, tuple(acc))
            for t in range(4):
                cols = pl.ds(pl.multiple_of(base + t * 128, 128), 128)
                cpart[v, :, cols] = acc[t]
            return carry

        lax.fori_loop(0, 4, step, 0)

    scores(1 - c, False, 0, 2)
    first_a = columns_start(0, 0)
    scores(1 - c, False, 2, 4)
    first_b = columns_start(0, 1)
    for it in range(2):
        first_a()
        second_a = columns_next(it, 0)
        first_b()
        second_b = columns_next(it, 1)
        second_a()
        columns_end(it, 0)
        row_pass(it, 0)
        second_b()
        columns_end(it, 1)
        row_pass(it, 1)
        got_rows = row_start(it)
        if it == 0:
            got_rows()
            row_end(it)
            column_pass(0)
            first_a = columns_start(1, 0)
            column_pass(1)
            first_b = columns_start(1, 1)

    def scaled(i, carry):
        q = lax.div(i, 4)
        v = lax.rem(q, 2)
        rows = pl.ds(pl.multiple_of(lax.rem(i, 4) * 32, 32), 32)
        zr = zb[q, rows, :]
        for t in range(COLS // 128):
            cols = slice(t * 128, (t + 1) * 128)
            e = e_ref[q, rows, cols]
            m_ref[q, rows, cols] = e * e * cvec[v, t : t + 1, :]
            e_ref[q, rows, cols] = e * zr
        return carry

    lax.fori_loop(0, 16, scaled, 0)

    to = lax.broadcasted_iota(jnp.int32, (D, D), 0)
    at = lax.broadcasted_iota(jnp.int32, (D, D), 1)
    natural = (to == at).astype(BF16)
    swapped = ((to // 32) * 4 + ((to // 4) % 8) * 32 + to % 4 == at).astype(BF16)
    for h, order in ((0, natural), (1, swapped)):
        for slot in range(2):
            ut[h, :, slot * 256 : (slot + 1) * 256] = lax.dot_general(
                order, uall[slot], (((1,), (1,)), ((), ())), preferred_element_type=F32
            ).astype(BF16)

    got_rows()
    row_end(1)

    chunks = []
    for j in range(HALF // CH):
        sign = 1 if j % 2 == 0 else -1
        chunks.append(("y", "z", 0, j * CH, sign))
        chunks.append(("z", "y", 1, HALF + j * CH, sign))
    own = {"y": y, "z": z}

    def slab(ch, s):
        which = lax.rem(own[chunks[ch][0]] + (s + RING), RING)
        return gpart.at[ch, pl.ds(pl.multiple_of(which * 32, 32), 32), :]

    flight = {}

    def hop(ch, way, src, s):
        flight[ch, way] = send(src, rs_recv.at[ch, way], along(chunks[ch][0], s % RING))

    def step0(ch):
        sign = chunks[ch][4]
        hop(ch, 6, slab(ch, 4 * sign), 2 * sign)
        hop(ch, 0, slab(ch, 3 * sign), sign)
        hop(ch, 3, slab(ch, -3 * sign), -sign)

    def step1(ch):
        sign = chunks[ch][4]
        flight[ch, 3]()
        here = rs_recv.at[ch, 3]
        here[...] = here[...] + slab(ch, -2 * sign)[...]
        hop(ch, 4, here, -sign)
        flight[ch, 0]()
        flight[ch, 6]()
        here = rs_recv.at[ch, 0]
        here[...] = here[...] + rs_recv[ch, 6] + slab(ch, 2 * sign)[...]
        hop(ch, 1, here, sign)

    def step2(ch):
        for way, sign in ((1, chunks[ch][4]), (4, -chunks[ch][4])):
            flight[ch, way]()
            here = rs_recv.at[ch, way]
            here[...] = here[...] + slab(ch, sign)[...]
            hop(ch, way + 1, here, sign)

    got_p2 = {}

    def step3(ch):
        axis2 = chunks[ch][1]
        flight[ch, 2]()
        flight[ch, 5]()
        total = slab(ch, 0)[...] + rs_recv[ch, 2] + rs_recv[ch, 5]
        for q in range(RING):
            p2send[ch, q] = total[q * 4 : q * 4 + 4, :]
        got_p2[ch] = fan(
            [
                (p2send.at[ch, lax.rem(own[axis2] + s, RING)], p2recv.at[ch, s - 1], along(axis2, s))
                for s in ORDER
            ],
            p2recv.at[ch],
        )

    def terms(ch):
        for q in range(4):
            o = q + 1 - 2 * (q % 2)
            for t in range(CH // 128):
                cols = slice(chunks[ch][3] + t * 128, chunks[ch][3] + (t + 1) * 128)
                g_ref[q * 128 : (q + 1) * 128, cols] = (
                    e_ref[q, :, cols] - m_ref[o, :, cols] * rb[o]
                ).astype(BF16)

    terms(0)
    for ch, (_, _, h, col0, _) in enumerate(chunks):
        if ch + 1 < len(chunks):
            terms(ch + 1)
        gpart[ch] = jnp.dot(ut[h], g_ref[:, col0 : col0 + CH], preferred_element_type=F32)
        step0(ch)

    def back(slot):
        return lax.dot_general(
            g_ref[pl.ds(pl.multiple_of(slot * 256, 256), 256), :],
            pn[...],
            (((1,), (1,)), ((), ())),
            preferred_element_type=F32,
        )

    def along_x(s):
        return device(y, z, c, lax.rem(x + s, XS))

    gu_send[...] = back(1 - c)
    got_gu = send(gu_send, gu_recv, sibling)
    gx[...] = back(c).reshape(4, 64, 256)
    for ch in range(len(chunks) // 2):
        step1(ch)
    got_gu()
    gx[...] = gx[...] + gu_recv[...].reshape(4, 64, 256)
    got_gx = fan(
        [(gx.at[lax.rem(x + s, XS)], gx_recv.at[s - 1], along_x(s)) for s in (2, 1, 3)], gx_recv
    )
    for ch in range(len(chunks) // 2, len(chunks)):
        step1(ch)
    for ch in range(len(chunks)):
        step2(ch)
    for ch in range(len(chunks) // 2):
        step3(ch)

    got_gx()
    g = gx[x] + gx_recv[0] + gx_recv[1] + gx_recv[2]
    wide = emb_ref[x].astype(F32)
    inv = lax.rsqrt(jnp.mean(wide * wide, axis=-1, keepdims=True) + 1e-06)
    mean = jnp.mean(wide * g, axis=-1, keepdims=True)
    gef[x] = (g * inv - wide * (inv * inv * inv * mean)) * 0.0625
    got_ge = [send(gef.at[x], gef.at[x], along_x(s)) for s in (2, 1, 3)]

    for ch in range(len(chunks) // 2, len(chunks)):
        step3(ch)

    def second(ch):
        _, axis2, _, col0, _ = chunks[ch]
        got_p2[ch]()
        total = p2send[ch, own[axis2]]
        for s in range(RING - 1):
            total = total + p2recv[ch, s]
        for q in range(2):
            fin[q, :, col0 : col0 + CH] = total[q * 2 : q * 2 + 2, :]

    for ch in range(len(chunks)):
        second(ch)
    got_fin = send(fin.at[1 - c], fin_recv, sibling)
    gp_ref[:, pl.ds(pl.multiple_of(c * COLS, COLS), COLS)] = fin[c]
    for wait in got_ge:
        wait()
    ge_ref[...] = gef[...]
    got_fin()
    gp_ref[:, pl.ds(pl.multiple_of((1 - c) * COLS, COLS), COLS)] = fin_recv[...]

    for wait in ends:
        wait()
    assert used[0] <= SEMS


SEMS = 96


def shards(embeddings, prototypes):
    vmem = pl.BlockSpec(memory_space=pltpu.VMEM)
    ge, gp = pl.pallas_call(
        kernel,
        name="swap_step",
        out_shape=(
            jax.ShapeDtypeStruct((4, 64, D), F32),
            jax.ShapeDtypeStruct((2, 2 * COLS), F32),
        ),
        in_specs=[pl.BlockSpec(memory_space=pltpu.HBM)] * 2,
        out_specs=(vmem, vmem),
        scratch_shapes=[
            pltpu.VMEM((4, 64, D), BF16),
            pltpu.VMEM((D, COLS), BF16),
            pltpu.VMEM((D, COLS), BF16),
            pltpu.VMEM((256, D), F32),
            pltpu.VMEM((256, D), F32),
            pltpu.VMEM((2, 256, D), BF16),
            pltpu.VMEM((2, D, 512), BF16),
            pltpu.VMEM((4, 128, COLS), F32),
            pltpu.VMEM((4, 128, COLS), F32),
            pltpu.VMEM((2, 8, COLS), F32),
            pltpu.VMEM((2, 2, 2, 2, 8, 128), F32),
            pltpu.VMEM((2, 2, 2, RING - 1, 2, 8, 128), F32),
            pltpu.VMEM((2, 16, 128), F32),
            pltpu.VMEM((2, 4, 128, 128), F32),
            pltpu.VMEM((2, 8, 128), F32),
            pltpu.VMEM((2, 2 * XS - 1, 8, 128), F32),
            pltpu.VMEM((4, 128, 128), F32),
            pltpu.VMEM((4, 128, 128), F32),
            pltpu.VMEM((512, COLS), BF16),
            pltpu.VMEM((CHUNKS, D, CH), F32),
            pltpu.VMEM((CHUNKS, 7, 32, CH), F32),
            pltpu.VMEM((CHUNKS, RING, 4, CH), F32),
            pltpu.VMEM((CHUNKS, RING - 1, 4, CH), F32),
            pltpu.VMEM((2, 2, COLS), F32),
            pltpu.VMEM((2, COLS), F32),
            pltpu.VMEM((256, D), F32),
            pltpu.VMEM((256, D), F32),
            pltpu.VMEM((4, 64, D), F32),
            pltpu.VMEM((3, 64, D), F32),
            pltpu.VMEM((4, 64, D), F32),
            pltpu.SemaphoreType.DMA((2,)),
            pltpu.SemaphoreType.DMA((SEMS,)),
            pltpu.SemaphoreType.DMA((SEMS,)),
        ],
        compiler_params=pltpu.CompilerParams(
            collective_id=0, has_side_effects=True, vmem_limit_bytes=52 << 20
        ),
        cost_estimate=pl.CostEstimate(
            flops=2_000_000_000, bytes_accessed=4_000_000, transcendentals=1_100_000
        ),
    )(embeddings.reshape(4, 64, D), prototypes)
    return ge.reshape(2, 128, D), gp


def solution(mesh):
    return jax.shard_map(
        shards,
        mesh=mesh,
        in_specs=(P(None, "dp", None), P(None, "proto")),
        out_specs=(P(None, "dp", None), P("dp", "proto")),
        check_vma=False,
    )
```
